32 devices in a mesh: win: 1, col: 32 (over z, y, x, core).
Axes of the slice: x: 2, y: 2, z: 4, core: 2. Of those that a mesh axis runs over, the one named last changes fastest.
Arguments:
- records: bfloat16 [1024, 2048], P('win', 'col'), may hold values from -6 to 6
- quality_mask: int32 [1024], P('win'), may hold values 0 or 1
- band_start: int32 [1], P('win'), may hold values from 0 to 512
Outputs:
- correlations: bfloat16 [512, 1024, 256], P('win', 'col')
The draws below stay inside these ranges and needn't reach their ends.
Inputs may be any that keep to these rules, and one draw needn't show every extreme that they name: `band_start`: the band lies inside the array.
All inputs are finite; a program needn't handle non-finite values.
Results may differ from the reference program's by a relative error of at most 0.0074.
Values may be sent and summed in bfloat16 or wider, within the bound.
A program may use at most 64 MiB of HBM per device.

```python
import jax
import jax.numpy as jnp
from jax import lax

L = 1024
LAGS = 256
SEG = 2
ROWS = 512
CH = 1024
F = 512
TIME = 2048


def set_ends(values, rng, smallest, top_value):
    longest = values.shape.index(max(values.shape))
    spots = []
    for shift in (0, 1):
        where = [jax.random.randint(jax.random.fold_in(rng, axis), (), 0, length) for axis, length in enumerate(values.shape)]
        where[longest] = (where[longest] + shift) % values.shape[longest]
        spots.append(tuple(where))
    return values.at[spots[0]].set(smallest).at[spots[1]].set(top_value)


def level_of(own_key, dims, pieces, smallest, high):
    def one(position, blocks):
        draws = jax.random.uniform(jax.random.fold_in(jax.random.fold_in(own_key, 6), position), (blocks,), jnp.float32, smallest / len(pieces), high / len(pieces))
        return jnp.repeat(jnp.exp(draws), dims[position] // blocks).reshape((-1,) + (1,) * (len(dims) - position - 1))

    loudness = one(*pieces[0])
    for cut in pieces[1:]:
        loudness = loudness * one(*cut)
    return loudness


def noise(rng, extent, width, limit, split=(), kind=jnp.bfloat16):
    entries = jax.random.normal(rng, extent, jnp.float32) * width
    if len(split) > 0:
        entries = level_of(rng, extent, split, -0.22, 0.18) * entries
    return jnp.clip(entries, min=-limit, max=limit).astype(kind)


def setup_inputs(seed: int = 0, part: int = 0) -> dict:
    keys = jax.random.split(jax.random.key(seed), 4)
    own_keys = jax.random.split(jax.random.fold_in(keys[3], part), 4)
    return {
        "records": noise(own_keys[0], (CH, TIME), 1.0, 6.0, ((1, 32),)),
        "quality_mask": set_ends((jax.random.randint(own_keys[1], (CH,), 0, 8) < 7).astype(jnp.int32), jax.random.fold_in(own_keys[1], 1), 0, 1),
        "band_start": jax.random.randint(own_keys[2], (1,), 0, CH - ROWS + 1).astype(jnp.int32),
    }


def dft_tables():
    sample_ids = jnp.arange(L, dtype=jnp.int32)
    bin_ids = jnp.arange(F, dtype=jnp.int32)
    phase = jnp.mod(sample_ids[:, None] * bin_ids[None, :], L).astype(jnp.float32) * (2.0 * jnp.pi / L)
    forward = jnp.concatenate([jnp.cos(phase), -jnp.sin(phase)], axis=1).astype(jnp.bfloat16)
    shifts = jnp.arange(LAGS, dtype=jnp.int32) - LAGS // 2
    turns = jnp.mod(bin_ids[:, None] * shifts[None, :], L).astype(jnp.float32) * (2.0 * jnp.pi / L)
    factor = 1.0 / jnp.sqrt(jnp.float32(SEG * F))
    inverse = (jnp.concatenate([jnp.cos(turns), -jnp.sin(turns)], axis=0) * factor).astype(jnp.bfloat16)
    return (forward, inverse)

def whitened_spectra(samples, forward):
    channels_here = samples.shape[0]
    spectra = jnp.dot(samples.reshape(channels_here * SEG, L), forward, preferred_element_type=jnp.float32)
    spectra = spectra.reshape(channels_here, SEG, 2 * F)
    real_part = spectra[:, :, :F]
    imag_part = spectra[:, :, F:]
    power_mean = lax.optimization_barrier(jnp.mean(real_part * real_part + imag_part * imag_part, axis=1))
    level_mean = lax.optimization_barrier(jnp.mean(power_mean, axis=1, keepdims=True))
    scaling = jnp.sqrt(power_mean + level_mean + 1e-06)
    return spectra / jnp.concatenate([scaling, scaling], axis=1)[:, None, :]

def correlate(band_row, white, inverse):
    row_values = band_row.astype(jnp.float32)
    col_values = white.astype(jnp.float32)
    row_real = row_values[None, :, :F]
    row_imag = row_values[None, :, F:]
    col_real = col_values[:, :, :F]
    col_imag = col_values[:, :, F:]
    cross_real = lax.optimization_barrier(jnp.sum(row_real * col_real + row_imag * col_imag, axis=1))
    cross_imag = lax.optimization_barrier(jnp.sum(row_imag * col_real - row_real * col_imag, axis=1))
    cross = jnp.concatenate([cross_real, cross_imag], axis=1).astype(jnp.bfloat16)
    return jnp.dot(cross, inverse, preferred_element_type=jnp.float32).astype(jnp.bfloat16)

def reference(records, quality_mask, band_start):
    forward, inverse = dft_tables()
    keep = quality_mask.astype(jnp.float32)[:, None, None]
    white = (whitened_spectra(records, forward) * keep).astype(jnp.bfloat16)
    band = lax.dynamic_slice_in_dim(white, band_start[0].astype(jnp.int32), ROWS, 0)
    return lax.map(lambda band_row: correlate(band_row, white, inverse), band)
```

```python
import functools

import jax
import jax.numpy as jnp
import numpy as np
from jax import lax
from jax.experimental import pallas as pl
from jax.experimental.pallas import tpu as pltpu
from jax.sharding import PartitionSpec as P

L = 1024
LAGS = 256
SEG = 2
ROWS = 512
F = 512
SUB = 8


def dft_tables():
    t = np.arange(L)
    f = np.arange(F)
    phase = np.mod(t[:, None] * f[None, :], L) * (2.0 * np.pi / L)
    forward = np.concatenate([np.cos(phase), -np.sin(phase)], axis=1).astype(np.float32)
    shifts = np.arange(LAGS) - LAGS // 2
    turns = np.mod(f[:, None] * shifts[None, :], L) * (2.0 * np.pi / L)
    inverse = np.concatenate([np.cos(turns), -np.sin(turns)], axis=0) / np.sqrt(SEG * F)
    return forward.astype(jnp.bfloat16), inverse.astype(np.float32).astype(jnp.bfloat16)


def whiten(sp0, sp1, keep):
    re0, im0, re1, im1 = sp0[:, :F], sp0[:, F:], sp1[:, :F], sp1[:, F:]
    power = ((re0 * re0 + im0 * im0) + (re1 * re1 + im1 * im1)) * (1.0 / SEG)
    level = jnp.mean(power, axis=1, keepdims=True)
    scale = lax.rsqrt(power + level + 1e-06) * keep
    return [(part * scale).astype(jnp.bfloat16) for part in (re0, im0, re1, im1)]


def correlate_kernel(
    channels, xb_ref, xo_ref, kb_ref, ko_ref, fwd_ref, inv_ref, out_ref,
    wb, wo, cross_a, cross_b, out_buf, sems,
):
    groups = channels // 16
    dot0 = functools.partial(
        lax.dot_general, dimension_numbers=(((0,), (0,)), ((), ())),
        preferred_element_type=jnp.float32,
    )
    own = [
        jnp.dot(xo_ref[:, s * L:(s + 1) * L], fwd_ref[...], preferred_element_type=jnp.float32)
        for s in range(SEG)
    ]
    for q, part in enumerate(whiten(own[0], own[1], ko_ref[...])):
        wo[:, q * F:(q + 1) * F] = part

    width = 256

    @pl.loop(0, ROWS // width)
    def _(i):
        cols = pl.ds(pl.multiple_of(i * width, width), width)
        band = [dot0(xb_ref[s * L:(s + 1) * L, cols], fwd_ref[...]) for s in range(SEG)]
        for q, part in enumerate(whiten(band[0], band[1], kb_ref[cols, :])):
            wb[cols, q * F:(q + 1) * F] = part.astype(jnp.float32)

    def cross(base, buf):
        for j in range(F // 128):
            lanes = [slice(q * F + j * 128, q * F + (j + 1) * 128) for q in range(4)]
            cols = [[wo[g * 16:(g + 1) * 16, lane] for lane in lanes] for g in range(groups)]
            rows8 = [wb[pl.ds(pl.multiple_of(base, SUB), SUB), lane] for lane in lanes]
            for i in range(SUB):
                a0, b0, a1, b1 = [
                    jnp.broadcast_to(tile[i:i + 1, :], (16, 128)).astype(jnp.bfloat16)
                    for tile in rows8
                ]
                for g in range(groups):
                    c0, d0, c1, d1 = cols[g]
                    real = (a0 * c0 + b0 * d0) + (a1 * c1 + b1 * d1)
                    imag = (b0 * c0 - a0 * d0) + (b1 * c1 - a1 * d1)
                    rows = slice(i * channels + g * 16, i * channels + (g + 1) * 16)
                    buf[rows, j * 128:(j + 1) * 128] = real
                    buf[rows, F + j * 128:F + (j + 1) * 128] = imag

    def lags(base, buf):
        res = jnp.dot(buf[...], inv_ref[...], preferred_element_type=jnp.float32)
        out_buf[pl.ds(pl.multiple_of(base, SUB), SUB)] = res.astype(jnp.bfloat16).reshape(SUB, channels, LAGS)

    def copy_out(k):
        rows = pl.ds(k * 2 * SUB, 2 * SUB)
        return pltpu.make_async_copy(out_buf.at[rows], out_ref.at[rows], sems.at[k])

    steps = ROWS // (2 * SUB)
    cross(0, cross_a)

    @pl.loop(0, steps)
    def _(k):
        base = k * 2 * SUB
        lags(base, cross_a)
        cross(base + SUB, cross_b)
        lags(base + SUB, cross_b)
        cross(jnp.minimum(base + 2 * SUB, ROWS - SUB), cross_a)
        copy_out(k).start()

    @pl.loop(0, steps)
    def _(k):
        copy_out(k).wait()


def on_device(records, quality_mask, band_start):
    devices_col = lax.axis_size("col")
    position = lax.axis_index("col")
    channels = records.shape[0] // devices_col
    forward, inverse = dft_tables()
    first_row = band_start[0]
    slab = lax.dynamic_slice_in_dim(records.T, first_row, ROWS, 1)
    band = lax.all_gather(slab, "col", axis=0, tiled=True)
    own = lax.all_to_all(records, "col", split_axis=0, concat_axis=1, tiled=True)
    mask = quality_mask.astype(jnp.float32)
    keep_band = lax.dynamic_slice_in_dim(mask, first_row, ROWS, 0)[:, None]
    keep_own = lax.dynamic_slice_in_dim(mask, position * channels, channels, 0)[:, None]
    vmem = pl.BlockSpec(memory_space=pltpu.VMEM)
    return pl.pallas_call(
        functools.partial(correlate_kernel, channels),
        out_shape=jax.ShapeDtypeStruct((ROWS, channels, LAGS), jnp.bfloat16),
        in_specs=[vmem] * 6,
        out_specs=pl.BlockSpec(memory_space=pl.ANY),
        scratch_shapes=[
            pltpu.VMEM((ROWS, 4 * F), jnp.float32),
            pltpu.VMEM((channels, 4 * F), jnp.bfloat16),
            pltpu.VMEM((SUB * channels, 2 * F), jnp.bfloat16),
            pltpu.VMEM((SUB * channels, 2 * F), jnp.bfloat16),
            pltpu.VMEM((ROWS, channels, LAGS), jnp.bfloat16),
            pltpu.SemaphoreType.DMA((ROWS // (2 * SUB),)),
        ],
        compiler_params=pltpu.CompilerParams(vmem_limit_bytes=52 * 2**20),
    )(band, own, keep_band, keep_own, jnp.asarray(forward), jnp.asarray(inverse))


def solution(mesh):
    return jax.shard_map(
        on_device,
        mesh=mesh,
        in_specs=(P("win", "col"), P("win"), P("win")),
        out_specs=P("win", "col", None),
        check_vma=False,
    )
```

```python
import functools

import jax
import jax.numpy as jnp
import numpy as np
from jax import lax
from jax.experimental import pallas as pl
from jax.experimental.pallas import tpu as pltpu
from jax.sharding import PartitionSpec as P

L = 1024
LAGS = 256
SEG = 2
ROWS = 512
F = 512
SUB = 8


def dft_tables():
    t = np.arange(L)
    f = np.arange(F)
    phase = np.mod(t[:, None] * f[None, :], L) * (2.0 * np.pi / L)
    forward = np.concatenate([np.cos(phase), -np.sin(phase)], axis=1).astype(np.float32)
    shifts = np.arange(LAGS) - LAGS // 2
    turns = np.mod(f[:, None] * shifts[None, :], L) * (2.0 * np.pi / L)
    inverse = np.concatenate([np.cos(turns), -np.sin(turns)], axis=0) / np.sqrt(SEG * F)
    return forward.astype(jnp.bfloat16), inverse.astype(np.float32).astype(jnp.bfloat16)


def whiten(sp0, sp1, keep):
    re0, im0, re1, im1 = sp0[:, :F], sp0[:, F:], sp1[:, :F], sp1[:, F:]
    power = ((re0 * re0 + im0 * im0) + (re1 * re1 + im1 * im1)) * (1.0 / SEG)
    level = jnp.mean(power, axis=1, keepdims=True)
    scale = lax.rsqrt(power + level + 1e-06) * keep
    return [(part * scale).astype(jnp.bfloat16) for part in (re0, im0, re1, im1)]


def prep_kernel(channels, groups, start_ref, rec_ref, slab_ref, pack_ref):
    total = rec_ref.shape[1]
    rec = rec_ref[...].astype(jnp.float32)
    shifted = pltpu.roll(rec, lax.rem(total - start_ref[0], total), 1)
    for h in range(2):
        slab_ref[h] = shifted[:, h * ROWS // 2:(h + 1) * ROWS // 2].astype(jnp.bfloat16)
    lane = lax.broadcasted_iota(jnp.int32, (16, 128), 1)
    per_tile = 128 // channels
    for dest in range(total // channels):
        j, i = divmod(dest, per_tile)
        packed = jnp.zeros((16, 128), jnp.float32)
        for k in range(groups):
            piece = rec[16 * k:16 * (k + 1), 128 * j:128 * (j + 1)]
            if k != i:
                piece = pltpu.roll(piece, (channels * (k - i)) % 128, 1)
            inside = (lane >= channels * k) & (lane < channels * (k + 1))
            packed = jnp.where(inside, piece, packed)
        pack_ref[dest] = packed.astype(jnp.bfloat16)


def bit_orders(n):
    bits = [1 << b for b in range(n.bit_length() - 1)]
    down = bits[::-1]
    other = list(down)
    if len(bits) >= 4:
        other[-3], other[-2] = other[-2], other[-3]
    return down, other


def exchange_kernel(
    n, slab_ref, pack_ref, gath_ref, own_ref,
    send_sems, recv_sems, own_send, own_recv, local_sems,
):
    me = lax.axis_index("col")

    def flip(mask):
        index = me
        for b in range(n.bit_length()):
            if mask >> b & 1:
                index = index + (1 << b) * (1 - 2 * ((me // (1 << b)) % 2))
        return index

    barrier = pltpu.get_barrier_semaphore()

    @pl.loop(1, n)
    def _(d):
        pl.semaphore_signal(
            barrier, inc=1, device_id={"col": (me + d) % n}, device_id_type=pl.DeviceIdType.MESH
        )

    pl.semaphore_wait(barrier, n - 1)

    def piece(h, held, bit):
        slot = gath_ref.at[h, flip(held)]
        return pltpu.make_async_remote_copy(
            src_ref=slab_ref.at[h] if held == 0 else slot,
            dst_ref=slot,
            send_sem=send_sems.at[h, held ^ bit],
            recv_sem=recv_sems.at[h, held ^ bit],
            device_id={"col": flip(bit)},
            device_id_type=pl.DeviceIdType.MESH,
        )

    def arrival(h, mask):
        slot = gath_ref.at[h, flip(mask)]
        return pltpu.make_async_remote_copy(
            src_ref=slab_ref.at[h],
            dst_ref=slot,
            send_sem=send_sems.at[h, mask],
            recv_sem=recv_sems.at[h, mask],
            device_id={"col": flip(1)},
            device_id_type=pl.DeviceIdType.MESH,
        )

    def own_push(d):
        return pltpu.make_async_remote_copy(
            src_ref=pack_ref.at[(me + d) % n],
            dst_ref=own_ref.at[me],
            send_sem=own_send.at[d],
            recv_sem=own_recv.at[d],
            device_id={"col": (me + d) % n},
            device_id_type=pl.DeviceIdType.MESH,
        )

    def own_arrival(d):
        return pltpu.make_async_remote_copy(
            src_ref=pack_ref.at[0],
            dst_ref=own_ref.at[(me - d + n) % n],
            send_sem=own_send.at[d],
            recv_sem=own_recv.at[d],
            device_id={"col": (me + d) % n},
            device_id_type=pl.DeviceIdType.MESH,
        )

    local = [pltpu.make_async_copy(slab_ref.at[h], gath_ref.at[h, me], local_sems.at[h]) for h in range(2)]
    local.append(pltpu.make_async_copy(pack_ref.at[me], own_ref.at[me], local_sems.at[2]))

    orders = bit_orders(n)
    held = [[0], [0]]
    waited = [set(), set()]
    started = []
    for stage in range(len(orders[0])):
        for pos in range(len(held[0])):
            for h in range(2):
                mask, bit = held[h][pos], orders[h][stage]
                if mask and mask not in waited[h]:
                    arrival(h, mask).wait_recv()
                    waited[h].add(mask)
                copy = piece(h, mask, bit)
                copy.start()
                started.append(copy)
        for h in range(2):
            held[h] = held[h] + [mask ^ orders[h][stage] for mask in held[h]]
        if stage == 0:
            for copy in local:
                copy.start()

            @pl.loop(1, n)
            def _(d):
                own_push(d).start()

    for h in range(2):
        for mask in held[h]:
            if mask and mask not in waited[h]:
                arrival(h, mask).wait_recv()
    for copy in started:
        copy.wait_send()
    for copy in local:
        copy.wait()

    @pl.loop(1, n)
    def _(d):
        own_push(d).wait_send()
        own_arrival(d).wait_recv()


def correlate_kernel(
    channels, xb_ref, xo_ref, kb_ref, ko_ref, fwd_ref, inv_ref, out_ref,
    wb, wo, cross_a, cross_b, out_buf, sems,
):
    groups = channels // 16
    dot0 = functools.partial(
        lax.dot_general, dimension_numbers=(((0,), (0,)), ((), ())),
        preferred_element_type=jnp.float32,
    )
    half = xo_ref.shape[0] // SEG
    table = fwd_ref[...].reshape(half, L // half, 2 * F)
    own = []
    for s in range(SEG):
        samples = xo_ref[s * half:(s + 1) * half].reshape(half * 16, 128)
        own.append(jnp.zeros((channels, 2 * F), jnp.float32))
        for k in range(L // half // 16):
            rows = table[:, 16 * k:16 * (k + 1), :].reshape(half * 16, 2 * F)
            own[s] += dot0(samples, rows)[channels * k:channels * (k + 1)]
    for q, part in enumerate(whiten(own[0], own[1], ko_ref[...])):
        wo[:, q * F:(q + 1) * F] = part

    width = ROWS // 2

    @pl.loop(0, 2)
    def _(i):
        cols = pl.ds(pl.multiple_of(i * width, width), width)
        band = [dot0(xb_ref[i, s * L:(s + 1) * L, :], fwd_ref[...]) for s in range(SEG)]
        for q, part in enumerate(whiten(band[0], band[1], kb_ref[cols, :])):
            wb[cols, q * F:(q + 1) * F] = part.astype(jnp.float32)

    def cross(base, buf):
        for j in range(F // 128):
            lanes = [slice(q * F + j * 128, q * F + (j + 1) * 128) for q in range(4)]
            cols = [[wo[g * 16:(g + 1) * 16, lane] for lane in lanes] for g in range(groups)]
            rows8 = [wb[pl.ds(pl.multiple_of(base, SUB), SUB), lane] for lane in lanes]
            for i in range(SUB):
                a0, b0, a1, b1 = [
                    jnp.broadcast_to(tile[i:i + 1, :], (16, 128)).astype(jnp.bfloat16)
                    for tile in rows8
                ]
                for g in range(groups):
                    c0, d0, c1, d1 = cols[g]
                    real = (a0 * c0 + b0 * d0) + (a1 * c1 + b1 * d1)
                    imag = (b0 * c0 - a0 * d0) + (b1 * c1 - a1 * d1)
                    rows = slice(i * channels + g * 16, i * channels + (g + 1) * 16)
                    buf[rows, j * 128:(j + 1) * 128] = real
                    buf[rows, F + j * 128:F + (j + 1) * 128] = imag

    def lags(base, buf):
        res = jnp.dot(buf[...], inv_ref[...], preferred_element_type=jnp.float32)
        out_buf[pl.ds(pl.multiple_of(base, SUB), SUB)] = res.astype(jnp.bfloat16).reshape(SUB, channels, LAGS)

    def copy_out(k):
        rows = pl.ds(k * 2 * SUB, 2 * SUB)
        return pltpu.make_async_copy(out_buf.at[rows], out_ref.at[rows], sems.at[k])

    steps = ROWS // (2 * SUB)
    cross(0, cross_a)

    @pl.loop(0, steps)
    def _(k):
        base = k * 2 * SUB
        lags(base, cross_a)
        cross(base + SUB, cross_b)
        lags(base + SUB, cross_b)
        cross(jnp.minimum(base + 2 * SUB, ROWS - SUB), cross_a)
        copy_out(k).start()

    @pl.loop(0, steps)
    def _(k):
        copy_out(k).wait()


def on_device(records, quality_mask, band_start):
    devices_col = lax.axis_size("col")
    position = lax.axis_index("col")
    channels = records.shape[0] // devices_col
    forward, inverse = dft_tables()
    first_row = band_start[0]
    local_time = records.shape[1]
    groups = local_time // 16
    n = devices_col
    vmem = pl.BlockSpec(memory_space=pltpu.VMEM)
    hbm = pl.BlockSpec(memory_space=pl.ANY)
    slab, pack = pl.pallas_call(
        functools.partial(prep_kernel, channels, groups),
        out_shape=(
            jax.ShapeDtypeStruct((2, local_time, ROWS // 2), jnp.bfloat16),
            jax.ShapeDtypeStruct((n, 16, 128), jnp.bfloat16),
        ),
        in_specs=[pl.BlockSpec(memory_space=pltpu.SMEM), vmem],
        out_specs=(vmem, vmem),
    )(band_start, records.T)
    band, own = pl.pallas_call(
        functools.partial(exchange_kernel, n),
        out_shape=(
            jax.ShapeDtypeStruct((2, n, local_time, ROWS // 2), jnp.bfloat16),
            jax.ShapeDtypeStruct((n, 16, 128), jnp.bfloat16),
        ),
        in_specs=[hbm, hbm],
        out_specs=(hbm, hbm),
        scratch_shapes=[
            pltpu.SemaphoreType.DMA((2, n)),
            pltpu.SemaphoreType.DMA((2, n)),
            pltpu.SemaphoreType.DMA((n,)),
            pltpu.SemaphoreType.DMA((n,)),
            pltpu.SemaphoreType.DMA((3,)),
        ],
        compiler_params=pltpu.CompilerParams(collective_id=0, has_side_effects=True),
    )(slab, pack)
    band = band.reshape(2, n * local_time, ROWS // 2)
    mask = quality_mask.astype(jnp.float32)
    keep_band = lax.dynamic_slice_in_dim(mask, first_row, ROWS, 0)[:, None]
    keep_own = lax.dynamic_slice_in_dim(mask, position * channels, channels, 0)[:, None]
    return pl.pallas_call(
        functools.partial(correlate_kernel, channels),
        out_shape=jax.ShapeDtypeStruct((ROWS, channels, LAGS), jnp.bfloat16),
        in_specs=[vmem] * 6,
        out_specs=pl.BlockSpec(memory_space=pl.ANY),
        scratch_shapes=[
            pltpu.VMEM((ROWS, 4 * F), jnp.float32),
            pltpu.VMEM((channels, 4 * F), jnp.bfloat16),
            pltpu.VMEM((SUB * channels, 2 * F), jnp.bfloat16),
            pltpu.VMEM((SUB * channels, 2 * F), jnp.bfloat16),
            pltpu.VMEM((ROWS, channels, LAGS), jnp.bfloat16),
            pltpu.SemaphoreType.DMA((ROWS // (2 * SUB),)),
        ],
        compiler_params=pltpu.CompilerParams(vmem_limit_bytes=52 * 2**20),
    )(band, own, keep_band, keep_own, jnp.asarray(forward), jnp.asarray(inverse))


def solution(mesh):
    return jax.shard_map(
        on_device,
        mesh=mesh,
        in_specs=(P("win", "col"), P("win"), P("win")),
        out_specs=P("win", "col", None),
        check_vma=False,
    )
```

```python
import functools

import jax
import jax.numpy as jnp
import numpy as np
from jax import lax
from jax.experimental import pallas as pl
from jax.experimental.pallas import tpu as pltpu
from jax.sharding import PartitionSpec as P

L = 1024
LAGS = 256
SEG = 2
ROWS = 512
F = 512
SUB = 16


def dft_tables():
    t = np.arange(L)
    f = np.arange(F)
    phase = np.mod(t[:, None] * f[None, :], L) * (2.0 * np.pi / L)
    forward = np.concatenate([np.cos(phase), -np.sin(phase)], axis=1).astype(np.float32)
    shifts = np.arange(LAGS) - LAGS // 2
    turns = np.mod(f[:, None] * shifts[None, :], L) * (2.0 * np.pi / L)
    inverse = np.concatenate([np.cos(turns), -np.sin(turns)], axis=0) / np.sqrt(SEG * F)
    return forward.astype(jnp.bfloat16), inverse.astype(np.float32).astype(jnp.bfloat16)


def whiten(sp0, sp1, keep):
    re0, im0, re1, im1 = sp0[:, :F], sp0[:, F:], sp1[:, :F], sp1[:, F:]
    power = ((re0 * re0 + im0 * im0) + (re1 * re1 + im1 * im1)) * (1.0 / SEG)
    level = jnp.mean(power, axis=1, keepdims=True)
    scale = lax.rsqrt(power + level + 1e-06) * keep
    return [(part * scale).astype(jnp.bfloat16) for part in (re0, im0, re1, im1)]


def prep_kernel(channels, groups, start_ref, rec_ref, slab_ref, pack_ref):
    total = rec_ref.shape[1]
    rec = rec_ref[...].astype(jnp.float32)
    shifted = pltpu.roll(rec, lax.rem(total - start_ref[0], total), 1)
    for h in range(2):
        slab_ref[h] = shifted[:, h * ROWS // 2:(h + 1) * ROWS // 2].astype(jnp.bfloat16)
    lane = lax.broadcasted_iota(jnp.int32, (16, 128), 1)
    per_tile = 128 // channels
    for dest in range(total // channels):
        j, i = divmod(dest, per_tile)
        packed = jnp.zeros((16, 128), jnp.float32)
        for k in range(groups):
            piece = rec[16 * k:16 * (k + 1), 128 * j:128 * (j + 1)]
            if k != i:
                piece = pltpu.roll(piece, (channels * (k - i)) % 128, 1)
            inside = (lane >= channels * k) & (lane < channels * (k + 1))
            packed = jnp.where(inside, piece, packed)
        pack_ref[dest] = packed.astype(jnp.bfloat16)


def bit_orders(n):
    bits = [1 << b for b in range(n.bit_length() - 1)]
    down = bits[::-1]
    other = list(down)
    if len(bits) >= 4:
        other[-3], other[-2] = other[-2], other[-3]
    return down, other


def exchange_kernel(
    n, slab_ref, pack_ref, gath_ref, own_ref,
    send_sems, recv_sems, own_send, own_recv, local_sems,
):
    me = lax.axis_index("col")

    def flip(mask):
        index = me
        for b in range(n.bit_length()):
            if mask >> b & 1:
                index = index + (1 << b) * (1 - 2 * ((me // (1 << b)) % 2))
        return index

    barrier = pltpu.get_barrier_semaphore()

    @pl.loop(1, n)
    def _(d):
        pl.semaphore_signal(
            barrier, inc=1, device_id={"col": (me + d) % n}, device_id_type=pl.DeviceIdType.MESH
        )

    pl.semaphore_wait(barrier, n - 1)

    def piece(h, held, bit):
        slot = gath_ref.at[h, flip(held)]
        return pltpu.make_async_remote_copy(
            src_ref=slab_ref.at[h] if held == 0 else slot,
            dst_ref=slot,
            send_sem=send_sems.at[h, held ^ bit],
            recv_sem=recv_sems.at[h, held ^ bit],
            device_id={"col": flip(bit)},
            device_id_type=pl.DeviceIdType.MESH,
        )

    def arrival(h, mask):
        slot = gath_ref.at[h, flip(mask)]
        return pltpu.make_async_remote_copy(
            src_ref=slab_ref.at[h],
            dst_ref=slot,
            send_sem=send_sems.at[h, mask],
            recv_sem=recv_sems.at[h, mask],
            device_id={"col": flip(1)},
            device_id_type=pl.DeviceIdType.MESH,
        )

    def own_push(d):
        return pltpu.make_async_remote_copy(
            src_ref=pack_ref.at[(me + d) % n],
            dst_ref=own_ref.at[me],
            send_sem=own_send.at[d],
            recv_sem=own_recv.at[d],
            device_id={"col": (me + d) % n},
            device_id_type=pl.DeviceIdType.MESH,
        )

    def own_arrival(d):
        return pltpu.make_async_remote_copy(
            src_ref=pack_ref.at[0],
            dst_ref=own_ref.at[(me - d + n) % n],
            send_sem=own_send.at[d],
            recv_sem=own_recv.at[d],
            device_id={"col": (me + d) % n},
            device_id_type=pl.DeviceIdType.MESH,
        )

    local = [pltpu.make_async_copy(slab_ref.at[h], gath_ref.at[h, me], local_sems.at[h]) for h in range(2)]
    local.append(pltpu.make_async_copy(pack_ref.at[me], own_ref.at[me], local_sems.at[2]))

    orders = bit_orders(n)
    held = [[0], [0]]
    waited = [set(), set()]
    started = []
    for stage in range(len(orders[0])):
        for h in range(2):
            held[h] = held[h] + [mask ^ orders[h][stage] for mask in held[h]]
    for pos in range(n // 2):
        for h in range(2):
            mask = held[h][pos]
            if mask:
                arrival(h, mask).wait_recv()
                waited[h].add(mask)
            for bit in orders[h][pos.bit_length():]:
                copy = piece(h, mask, bit)
                copy.start()
                started.append(copy)
        if pos == 0:
            for copy in local:
                copy.start()

            @pl.loop(1, n)
            def _(d):
                own_push(d).start()

    for h in range(2):
        for mask in held[h]:
            if mask and mask not in waited[h]:
                arrival(h, mask).wait_recv()
    for copy in started:
        copy.wait_send()
    for copy in local:
        copy.wait()

    @pl.loop(1, n)
    def _(d):
        own_push(d).wait_send()
        own_arrival(d).wait_recv()


def correlate_kernel(
    channels, xb_ref, xo_ref, kb_ref, ko_ref, fwd_ref, inv_ref, out_ref,
    wb, wo, cross_a, cross_b, out_buf, sems,
):
    groups = channels // 16
    dot0 = functools.partial(
        lax.dot_general, dimension_numbers=(((0,), (0,)), ((), ())),
        preferred_element_type=jnp.float32,
    )
    half = xo_ref.shape[0] // SEG
    table = fwd_ref[...].reshape(half, L // half, 2 * F)
    own = []
    for s in range(SEG):
        samples = xo_ref[s * half:(s + 1) * half].reshape(half * 16, 128)
        own.append(jnp.zeros((channels, 2 * F), jnp.float32))
        for k in range(L // half // 16):
            rows = table[:, 16 * k:16 * (k + 1), :].reshape(half * 16, 2 * F)
            own[s] += dot0(samples, rows)[channels * k:channels * (k + 1)]
    for q, part in enumerate(whiten(own[0], own[1], ko_ref[...])):
        wo[:, q * F:(q + 1) * F] = part

    width = ROWS // 2

    @pl.loop(0, 2)
    def _(i):
        cols = pl.ds(pl.multiple_of(i * width, width), width)
        band = [dot0(xb_ref[i, s * L:(s + 1) * L, :], fwd_ref[...]) for s in range(SEG)]
        for q, part in enumerate(whiten(band[0], band[1], kb_ref[cols, :])):
            wb[cols, q * F:(q + 1) * F] = part.astype(jnp.float32)

    def cross(base, buf):
        for j in range(F // 128):
            lanes = [slice(q * F + j * 128, q * F + (j + 1) * 128) for q in range(4)]
            cols = [[wo[g * 16:(g + 1) * 16, lane] for lane in lanes] for g in range(groups)]
            tiles = [wb[pl.ds(pl.multiple_of(base, SUB), SUB), lane] for lane in lanes]
            for i in range(SUB):
                a0, b0, a1, b1 = [
                    jnp.broadcast_to(tile[i:i + 1, :], (16, 128)).astype(jnp.bfloat16)
                    for tile in tiles
                ]
                for g in range(groups):
                    c0, d0, c1, d1 = cols[g]
                    real = (a0 * c0 + b0 * d0) + (a1 * c1 + b1 * d1)
                    imag = (b0 * c0 - a0 * d0) + (b1 * c1 - a1 * d1)
                    rows = slice(i * channels + g * 16, i * channels + (g + 1) * 16)
                    buf[rows, j * 128:(j + 1) * 128] = real
                    buf[rows, F + j * 128:F + (j + 1) * 128] = imag

    def lags(base, buf):
        res = jnp.dot(buf[...], inv_ref[...], preferred_element_type=jnp.float32)
        out_buf[pl.ds(pl.multiple_of(base, SUB), SUB)] = res.astype(jnp.bfloat16).reshape(SUB, channels, LAGS)

    def copy_out(k):
        rows = pl.ds(k * 2 * SUB, 2 * SUB)
        return pltpu.make_async_copy(out_buf.at[rows], out_ref.at[rows], sems.at[k])

    steps = ROWS // (2 * SUB)
    cross(0, cross_a)

    @pl.loop(0, steps)
    def _(k):
        base = k * 2 * SUB
        lags(base, cross_a)
        cross(base + SUB, cross_b)
        lags(base + SUB, cross_b)
        cross(jnp.minimum(base + 2 * SUB, ROWS - SUB), cross_a)
        copy_out(k).start()

    @pl.loop(0, steps)
    def _(k):
        copy_out(k).wait()


def on_device(records, quality_mask, band_start):
    devices_col = lax.axis_size("col")
    position = lax.axis_index("col")
    channels = records.shape[0] // devices_col
    forward, inverse = dft_tables()
    first_row = band_start[0]
    local_time = records.shape[1]
    groups = local_time // 16
    n = devices_col
    vmem = pl.BlockSpec(memory_space=pltpu.VMEM)
    hbm = pl.BlockSpec(memory_space=pl.ANY)
    slab, pack = pl.pallas_call(
        functools.partial(prep_kernel, channels, groups),
        out_shape=(
            jax.ShapeDtypeStruct((2, local_time, ROWS // 2), jnp.bfloat16),
            jax.ShapeDtypeStruct((n, 16, 128), jnp.bfloat16),
        ),
        in_specs=[pl.BlockSpec(memory_space=pltpu.SMEM), vmem],
        out_specs=(vmem, vmem),
    )(band_start, records.T)
    band, own = pl.pallas_call(
        functools.partial(exchange_kernel, n),
        out_shape=(
            jax.ShapeDtypeStruct((2, n, local_time, ROWS // 2), jnp.bfloat16),
            jax.ShapeDtypeStruct((n, 16, 128), jnp.bfloat16),
        ),
        in_specs=[hbm, hbm],
        out_specs=(hbm, hbm),
        scratch_shapes=[
            pltpu.SemaphoreType.DMA((2, n)),
            pltpu.SemaphoreType.DMA((2, n)),
            pltpu.SemaphoreType.DMA((n,)),
            pltpu.SemaphoreType.DMA((n,)),
            pltpu.SemaphoreType.DMA((3,)),
        ],
        compiler_params=pltpu.CompilerParams(collective_id=0, has_side_effects=True),
    )(slab, pack)
    band = band.reshape(2, n * local_time, ROWS // 2)
    mask = quality_mask.astype(jnp.float32)
    keep_band = lax.dynamic_slice_in_dim(mask, first_row, ROWS, 0)[:, None]
    keep_own = lax.dynamic_slice_in_dim(mask, position * channels, channels, 0)[:, None]
    return pl.pallas_call(
        functools.partial(correlate_kernel, channels),
        out_shape=jax.ShapeDtypeStruct((ROWS, channels, LAGS), jnp.bfloat16),
        in_specs=[vmem] * 6,
        out_specs=pl.BlockSpec(memory_space=pl.ANY),
        scratch_shapes=[
            pltpu.VMEM((ROWS, 4 * F), jnp.float32),
            pltpu.VMEM((channels, 4 * F), jnp.bfloat16),
            pltpu.VMEM((SUB * channels, 2 * F), jnp.bfloat16),
            pltpu.VMEM((SUB * channels, 2 * F), jnp.bfloat16),
            pltpu.VMEM((ROWS, channels, LAGS), jnp.bfloat16),
            pltpu.SemaphoreType.DMA((ROWS // (2 * SUB),)),
        ],
        compiler_params=pltpu.CompilerParams(vmem_limit_bytes=52 * 2**20),
    )(band, own, keep_band, keep_own, jnp.asarray(forward), jnp.asarray(inverse))


def solution(mesh):
    return jax.shard_map(
        on_device,
        mesh=mesh,
        in_specs=(P("win", "col"), P("win"), P("win")),
        out_specs=P("win", "col", None),
        check_vma=False,
    )
```

```python
import functools

import jax
import jax.numpy as jnp
import numpy as np
from jax import lax
from jax.experimental import pallas as pl
from jax.experimental.pallas import tpu as pltpu
from jax.sharding import PartitionSpec as P

L = 1024
LAGS = 256
SEG = 2
ROWS = 512
F = 512
SUB = 32


def dft_tables():
    t = np.arange(L)
    f = np.arange(F)
    phase = np.mod(t[:, None] * f[None, :], L) * (2.0 * np.pi / L)
    forward = np.concatenate([np.cos(phase), -np.sin(phase)], axis=1).astype(np.float32)
    shifts = np.arange(LAGS) - LAGS // 2
    turns = np.mod(f[:, None] * shifts[None, :], L) * (2.0 * np.pi / L)
    inverse = np.concatenate([np.cos(turns), -np.sin(turns)], axis=0) / np.sqrt(SEG * F)
    return forward.astype(jnp.bfloat16), inverse.astype(np.float32).astype(jnp.bfloat16)


def whiten(sp0, sp1, keep):
    re0, im0, re1, im1 = sp0[:, :F], sp0[:, F:], sp1[:, :F], sp1[:, F:]
    power = ((re0 * re0 + im0 * im0) + (re1 * re1 + im1 * im1)) * (1.0 / SEG)
    level = jnp.mean(power, axis=1, keepdims=True)
    scale = lax.rsqrt(power + level + 1e-06) * keep
    return [(part * scale).astype(jnp.bfloat16) for part in (re0, im0, re1, im1)]


def prep_kernel(channels, groups, start_ref, rec_ref, slab_ref, pack_ref):
    total = rec_ref.shape[1]
    rec = rec_ref[...].astype(jnp.float32)
    shifted = pltpu.roll(rec, lax.rem(total - start_ref[0], total), 1)
    for h in range(2):
        slab_ref[h] = shifted[:, h * ROWS // 2:(h + 1) * ROWS // 2].astype(jnp.bfloat16)
    lane = lax.broadcasted_iota(jnp.int32, (16, 128), 1)
    per_tile = 128 // channels
    for dest in range(total // channels):
        j, i = divmod(dest, per_tile)
        packed = jnp.zeros((16, 128), jnp.float32)
        for k in range(groups):
            piece = rec[16 * k:16 * (k + 1), 128 * j:128 * (j + 1)]
            if k != i:
                piece = pltpu.roll(piece, (channels * (k - i)) % 128, 1)
            inside = (lane >= channels * k) & (lane < channels * (k + 1))
            packed = jnp.where(inside, piece, packed)
        pack_ref[dest] = packed.astype(jnp.bfloat16)


def bit_orders(n):
    bits = [1 << b for b in range(n.bit_length() - 1)]
    down = bits[::-1]
    other = list(down)
    if len(bits) >= 4:
        other[-3], other[-2] = other[-2], other[-3]
    return down, other


def exchange_kernel(
    n, slab_ref, pack_ref, gath_ref, own_ref,
    send_sems, recv_sems, own_send, own_recv, local_sems,
):
    me = lax.axis_index("col")

    def flip(mask):
        index = me
        for b in range(n.bit_length()):
            if mask >> b & 1:
                index = index + (1 << b) * (1 - 2 * ((me // (1 << b)) % 2))
        return index

    barrier = pltpu.get_barrier_semaphore()

    @pl.loop(1, n)
    def _(d):
        pl.semaphore_signal(
            barrier, inc=1, device_id={"col": (me + d) % n}, device_id_type=pl.DeviceIdType.MESH
        )

    pl.semaphore_wait(barrier, n - 1)

    def piece(h, held, bit):
        slot = gath_ref.at[h, flip(held)]
        return pltpu.make_async_remote_copy(
            src_ref=slab_ref.at[h] if held == 0 else slot,
            dst_ref=slot,
            send_sem=send_sems.at[h, held ^ bit],
            recv_sem=recv_sems.at[h, held ^ bit],
            device_id={"col": flip(bit)},
            device_id_type=pl.DeviceIdType.MESH,
        )

    def arrival(h, mask):
        slot = gath_ref.at[h, flip(mask)]
        return pltpu.make_async_remote_copy(
            src_ref=slab_ref.at[h],
            dst_ref=slot,
            send_sem=send_sems.at[h, mask],
            recv_sem=recv_sems.at[h, mask],
            device_id={"col": flip(1)},
            device_id_type=pl.DeviceIdType.MESH,
        )

    def own_push(d):
        return pltpu.make_async_remote_copy(
            src_ref=pack_ref.at[(me + d) % n],
            dst_ref=own_ref.at[me],
            send_sem=own_send.at[d],
            recv_sem=own_recv.at[d],
            device_id={"col": (me + d) % n},
            device_id_type=pl.DeviceIdType.MESH,
        )

    def own_arrival(d):
        return pltpu.make_async_remote_copy(
            src_ref=pack_ref.at[0],
            dst_ref=own_ref.at[(me - d + n) % n],
            send_sem=own_send.at[d],
            recv_sem=own_recv.at[d],
            device_id={"col": (me + d) % n},
            device_id_type=pl.DeviceIdType.MESH,
        )

    local = [pltpu.make_async_copy(slab_ref.at[h], gath_ref.at[h, me], local_sems.at[h]) for h in range(2)]
    local.append(pltpu.make_async_copy(pack_ref.at[me], own_ref.at[me], local_sems.at[2]))

    orders = bit_orders(n)
    held = [[0], [0]]
    waited = [set(), set()]
    started = []
    for stage in range(len(orders[0])):
        for h in range(2):
            held[h] = held[h] + [mask ^ orders[h][stage] for mask in held[h]]
    for pos in range(n // 2):
        for h in range(2):
            mask = held[h][pos]
            if mask:
                arrival(h, mask).wait_recv()
                waited[h].add(mask)
            for bit in orders[h][pos.bit_length():]:
                copy = piece(h, mask, bit)
                copy.start()
                started.append(copy)
        if pos == 0:
            for copy in local:
                copy.start()
        if pos == n // 8 - 1:

            @pl.loop(1, n)
            def _(d):
                own_push(d).start()

    for h in range(2):
        for mask in held[h]:
            if mask and mask not in waited[h]:
                arrival(h, mask).wait_recv()
    for copy in started:
        copy.wait_send()
    for copy in local:
        copy.wait()

    @pl.loop(1, n)
    def _(d):
        own_push(d).wait_send()
        own_arrival(d).wait_recv()


def correlate_kernel(
    channels, xb_ref, xo_ref, kb_ref, ko_ref, fwd_ref, inv_ref, out_ref,
    wb, wo, cross_a, cross_b, out_buf, sems,
):
    groups = channels // 16
    dot0 = functools.partial(
        lax.dot_general, dimension_numbers=(((0,), (0,)), ((), ())),
        preferred_element_type=jnp.float32,
    )
    half = xo_ref.shape[0] // SEG
    table = fwd_ref[...].reshape(half, L // half, 2 * F)
    own = []
    for s in range(SEG):
        samples = xo_ref[s * half:(s + 1) * half].reshape(half * 16, 128)
        own.append(jnp.zeros((channels, 2 * F), jnp.float32))
        for k in range(L // half // 16):
            rows = table[:, 16 * k:16 * (k + 1), :].reshape(half * 16, 2 * F)
            own[s] += dot0(samples, rows)[channels * k:channels * (k + 1)]
    for q, part in enumerate(whiten(own[0], own[1], ko_ref[...])):
        wo[:, q * F:(q + 1) * F] = part

    width = ROWS // 2

    @pl.loop(0, 2)
    def _(i):
        cols = pl.ds(pl.multiple_of(i * width, width), width)
        band = [dot0(xb_ref[i, s * L:(s + 1) * L, :], fwd_ref[...]) for s in range(SEG)]
        for q, part in enumerate(whiten(band[0], band[1], kb_ref[cols, :])):
            wb[cols, q * F:(q + 1) * F] = part.astype(jnp.float32)

    def cross(base, buf):
        for j in range(F // 128):
            lanes = [slice(q * F + j * 128, q * F + (j + 1) * 128) for q in range(4)]
            cols = [[wo[g * 16:(g + 1) * 16, lane] for lane in lanes] for g in range(groups)]
            tiles = [wb[pl.ds(pl.multiple_of(base, SUB), SUB), lane] for lane in lanes]
            for i in range(SUB):
                a0, b0, a1, b1 = [
                    jnp.broadcast_to(tile[i:i + 1, :], (16, 128)).astype(jnp.bfloat16)
                    for tile in tiles
                ]
                for g in range(groups):
                    c0, d0, c1, d1 = cols[g]
                    real = (a0 * c0 + b0 * d0) + (a1 * c1 + b1 * d1)
                    imag = (b0 * c0 - a0 * d0) + (b1 * c1 - a1 * d1)
                    rows = slice(i * channels + g * 16, i * channels + (g + 1) * 16)
                    buf[rows, j * 128:(j + 1) * 128] = real
                    buf[rows, F + j * 128:F + (j + 1) * 128] = imag

    def lags(base, buf):
        res = jnp.dot(buf[...], inv_ref[...], preferred_element_type=jnp.float32)
        out_buf[pl.ds(pl.multiple_of(base, SUB), SUB)] = res.astype(jnp.bfloat16).reshape(SUB, channels, LAGS)

    def copy_out(k):
        rows = pl.ds(k * 2 * SUB, 2 * SUB)
        return pltpu.make_async_copy(out_buf.at[rows], out_ref.at[rows], sems.at[k])

    steps = ROWS // (2 * SUB)
    cross(0, cross_a)

    @pl.loop(0, steps)
    def _(k):
        base = k * 2 * SUB
        lags(base, cross_a)
        cross(base + SUB, cross_b)
        lags(base + SUB, cross_b)
        cross(jnp.minimum(base + 2 * SUB, ROWS - SUB), cross_a)
        copy_out(k).start()

    @pl.loop(0, steps)
    def _(k):
        copy_out(k).wait()


def on_device(records, quality_mask, band_start):
    devices_col = lax.axis_size("col")
    position = lax.axis_index("col")
    channels = records.shape[0] // devices_col
    forward, inverse = dft_tables()
    first_row = band_start[0]
    local_time = records.shape[1]
    groups = local_time // 16
    n = devices_col
    vmem = pl.BlockSpec(memory_space=pltpu.VMEM)
    hbm = pl.BlockSpec(memory_space=pl.ANY)
    slab, pack = pl.pallas_call(
        functools.partial(prep_kernel, channels, groups),
        out_shape=(
            jax.ShapeDtypeStruct((2, local_time, ROWS // 2), jnp.bfloat16),
            jax.ShapeDtypeStruct((n, 16, 128), jnp.bfloat16),
        ),
        in_specs=[pl.BlockSpec(memory_space=pltpu.SMEM), vmem],
        out_specs=(vmem, vmem),
    )(band_start, records.T)
    band, own = pl.pallas_call(
        functools.partial(exchange_kernel, n),
        out_shape=(
            jax.ShapeDtypeStruct((2, n, local_time, ROWS // 2), jnp.bfloat16),
            jax.ShapeDtypeStruct((n, 16, 128), jnp.bfloat16),
        ),
        in_specs=[hbm, hbm],
        out_specs=(hbm, hbm),
        scratch_shapes=[
            pltpu.SemaphoreType.DMA((2, n)),
            pltpu.SemaphoreType.DMA((2, n)),
            pltpu.SemaphoreType.DMA((n,)),
            pltpu.SemaphoreType.DMA((n,)),
            pltpu.SemaphoreType.DMA((3,)),
        ],
        compiler_params=pltpu.CompilerParams(collective_id=0, has_side_effects=True),
    )(slab, pack)
    band = band.reshape(2, n * local_time, ROWS // 2)
    mask = quality_mask.astype(jnp.float32)
    keep_band = lax.dynamic_slice_in_dim(mask, first_row, ROWS, 0)[:, None]
    keep_own = lax.dynamic_slice_in_dim(mask, position * channels, channels, 0)[:, None]
    return pl.pallas_call(
        functools.partial(correlate_kernel, channels),
        out_shape=jax.ShapeDtypeStruct((ROWS, channels, LAGS), jnp.bfloat16),
        in_specs=[vmem] * 6,
        out_specs=pl.BlockSpec(memory_space=pl.ANY),
        scratch_shapes=[
            pltpu.VMEM((ROWS, 4 * F), jnp.float32),
            pltpu.VMEM((channels, 4 * F), jnp.bfloat16),
            pltpu.VMEM((SUB * channels, 2 * F), jnp.bfloat16),
            pltpu.VMEM((SUB * channels, 2 * F), jnp.bfloat16),
            pltpu.VMEM((ROWS, channels, LAGS), jnp.bfloat16),
            pltpu.SemaphoreType.DMA((ROWS // (2 * SUB),)),
        ],
        compiler_params=pltpu.CompilerParams(vmem_limit_bytes=52 * 2**20),
    )(band, own, keep_band, keep_own, jnp.asarray(forward), jnp.asarray(inverse))


def solution(mesh):
    return jax.shard_map(
        on_device,
        mesh=mesh,
        in_specs=(P("win", "col"), P("win"), P("win")),
        out_specs=P("win", "col", None),
        check_vma=False,
    )
```

```python
import functools

import jax
import jax.numpy as jnp
import numpy as np
from jax import lax
from jax.experimental import pallas as pl
from jax.experimental.pallas import tpu as pltpu
from jax.sharding import PartitionSpec as P

L = 1024
LAGS = 256
SEG = 2
ROWS = 512
F = 512
SUB = 32


def dft_tables():
    t = np.arange(L)
    f = np.arange(F)
    phase = np.mod(t[:, None] * f[None, :], L) * (2.0 * np.pi / L)
    forward = np.concatenate([np.cos(phase), -np.sin(phase)], axis=1).astype(np.float32)
    shifts = np.arange(LAGS) - LAGS // 2
    turns = np.mod(f[:, None] * shifts[None, :], L) * (2.0 * np.pi / L)
    inverse = np.concatenate([np.cos(turns), -np.sin(turns)], axis=0) / np.sqrt(SEG * F)
    return forward.astype(jnp.bfloat16), inverse.astype(np.float32).astype(jnp.bfloat16)


def whiten(sp0, sp1, keep):
    re0, im0, re1, im1 = sp0[:, :F], sp0[:, F:], sp1[:, :F], sp1[:, F:]
    power = ((re0 * re0 + im0 * im0) + (re1 * re1 + im1 * im1)) * (1.0 / SEG)
    level = jnp.mean(power, axis=1, keepdims=True)
    scale = lax.rsqrt(power + level + 1e-06) * keep
    return [(part * scale).astype(jnp.bfloat16) for part in (re0, im0, re1, im1)]


def prep_kernel(channels, groups, start_ref, rec_ref, slab_ref, pack_ref):
    total = rec_ref.shape[1]
    rec = rec_ref[...].astype(jnp.float32)
    shifted = pltpu.roll(rec, lax.rem(total - start_ref[0], total), 1)
    for h in range(2):
        slab_ref[h] = shifted[:, h * ROWS // 2:(h + 1) * ROWS // 2].astype(jnp.bfloat16)
    lane = lax.broadcasted_iota(jnp.int32, (16, 128), 1)
    per_tile = 128 // channels
    for dest in range(total // channels):
        j, i = divmod(dest, per_tile)
        packed = jnp.zeros((16, 128), jnp.float32)
        for k in range(groups):
            piece = rec[16 * k:16 * (k + 1), 128 * j:128 * (j + 1)]
            if k != i:
                piece = pltpu.roll(piece, (channels * (k - i)) % 128, 1)
            inside = (lane >= channels * k) & (lane < channels * (k + 1))
            packed = jnp.where(inside, piece, packed)
        pack_ref[dest] = packed.astype(jnp.bfloat16)


def bit_orders(n):
    bits = [1 << b for b in range(n.bit_length() - 1)]
    down = bits[::-1]
    other = list(down)
    if len(bits) >= 4:
        other[-3], other[-2] = other[-2], other[-3]
    return down, other


def exchange_kernel(
    n, slab_ref, pack_ref, gath_ref, own_ref,
    send_sems, recv_sems, own_send, own_recv, local_sems,
):
    me = lax.axis_index("col")

    def flip(mask):
        index = me
        for b in range(n.bit_length()):
            if mask >> b & 1:
                index = index + (1 << b) * (1 - 2 * ((me // (1 << b)) % 2))
        return index

    barrier = pltpu.get_barrier_semaphore()

    @pl.loop(1, n)
    def _(d):
        pl.semaphore_signal(
            barrier, inc=1, device_id={"col": (me + d) % n}, device_id_type=pl.DeviceIdType.MESH
        )

    pl.semaphore_wait(barrier, n - 1)

    def piece(h, held, bit):
        slot = gath_ref.at[h, flip(held)]
        return pltpu.make_async_remote_copy(
            src_ref=slab_ref.at[h] if held == 0 else slot,
            dst_ref=slot,
            send_sem=send_sems.at[h, held ^ bit],
            recv_sem=recv_sems.at[h, held ^ bit],
            device_id={"col": flip(bit)},
            device_id_type=pl.DeviceIdType.MESH,
        )

    def arrival(h, mask):
        slot = gath_ref.at[h, flip(mask)]
        return pltpu.make_async_remote_copy(
            src_ref=slab_ref.at[h],
            dst_ref=slot,
            send_sem=send_sems.at[h, mask],
            recv_sem=recv_sems.at[h, mask],
            device_id={"col": flip(1)},
            device_id_type=pl.DeviceIdType.MESH,
        )

    def own_push(d):
        return pltpu.make_async_remote_copy(
            src_ref=pack_ref.at[(me + d) % n],
            dst_ref=own_ref.at[me],
            send_sem=own_send.at[d],
            recv_sem=own_recv.at[d],
            device_id={"col": (me + d) % n},
            device_id_type=pl.DeviceIdType.MESH,
        )

    def own_arrival(d):
        return pltpu.make_async_remote_copy(
            src_ref=pack_ref.at[0],
            dst_ref=own_ref.at[(me - d + n) % n],
            send_sem=own_send.at[d],
            recv_sem=own_recv.at[d],
            device_id={"col": (me + d) % n},
            device_id_type=pl.DeviceIdType.MESH,
        )

    local = [pltpu.make_async_copy(slab_ref.at[h], gath_ref.at[h, me], local_sems.at[h]) for h in range(2)]
    local.append(pltpu.make_async_copy(pack_ref.at[me], own_ref.at[me], local_sems.at[2]))

    orders = bit_orders(n)
    held = [[0], [0]]
    waited = [set(), set()]
    started = []
    for stage in range(len(orders[0])):
        for h in range(2):
            held[h] = held[h] + [mask ^ orders[h][stage] for mask in held[h]]
    for pos in range(n // 2):
        for h in range(2):
            mask = held[h][pos]
            if mask:
                arrival(h, mask).wait_recv()
                waited[h].add(mask)
            for bit in orders[h][pos.bit_length():]:
                copy = piece(h, mask, bit)
                copy.start()
                started.append(copy)
        if pos == 0:
            for copy in local:
                copy.start()
        if pos == n // 8 - 1:

            @pl.loop(1, n)
            def _(d):
                own_push(d).start()

    for h in range(2):
        for mask in held[h]:
            if mask and mask not in waited[h]:
                arrival(h, mask).wait_recv()
    for copy in started:
        copy.wait_send()
    for copy in local:
        copy.wait()

    @pl.loop(1, n)
    def _(d):
        own_push(d).wait_send()
        own_arrival(d).wait_recv()


def correlate_kernel(
    channels, xb_ref, xo_ref, kb_ref, ko_ref, fwd_ref, inv_ref, out_ref,
    wb, wo, cross_a, cross_b, out_buf, sems, xb, xb_sems,
):
    groups = channels // 16

    def copy_in(i):
        return pltpu.make_async_copy(xb_ref.at[i], xb.at[i], xb_sems.at[i])

    for i in range(2):
        copy_in(i).start()
    dot0 = functools.partial(
        lax.dot_general, dimension_numbers=(((0,), (0,)), ((), ())),
        preferred_element_type=jnp.float32,
    )
    half = xo_ref.shape[0] // SEG
    table = fwd_ref[...].reshape(half, L // half, 2 * F)
    own = []
    for s in range(SEG):
        samples = xo_ref[s * half:(s + 1) * half].reshape(half * 16, 128)
        own.append(jnp.zeros((channels, 2 * F), jnp.float32))
        for k in range(L // half // 16):
            rows = table[:, 16 * k:16 * (k + 1), :].reshape(half * 16, 2 * F)
            own[s] += dot0(samples, rows)[channels * k:channels * (k + 1)]
    for q, part in enumerate(whiten(own[0], own[1], ko_ref[...])):
        wo[:, q * F:(q + 1) * F] = part

    width = ROWS // 2

    @pl.loop(0, 2)
    def _(i):
        cols = pl.ds(pl.multiple_of(i * width, width), width)
        copy_in(i).wait()
        band = [dot0(xb[i, s * L:(s + 1) * L, :], fwd_ref[...]) for s in range(SEG)]
        for q, part in enumerate(whiten(band[0], band[1], kb_ref[cols, :])):
            wb[cols, q * F:(q + 1) * F] = part.astype(jnp.float32)

    def cross(base, buf):
        for j in range(F // 128):
            lanes = [slice(q * F + j * 128, q * F + (j + 1) * 128) for q in range(4)]
            cols = [[wo[g * 16:(g + 1) * 16, lane] for lane in lanes] for g in range(groups)]
            tiles = [wb[pl.ds(pl.multiple_of(base, SUB), SUB), lane] for lane in lanes]
            for i in range(SUB):
                a0, b0, a1, b1 = [
                    jnp.broadcast_to(tile[i:i + 1, :], (16, 128)).astype(jnp.bfloat16)
                    for tile in tiles
                ]
                for g in range(groups):
                    c0, d0, c1, d1 = cols[g]
                    real = (a0 * c0 + b0 * d0) + (a1 * c1 + b1 * d1)
                    imag = (b0 * c0 - a0 * d0) + (b1 * c1 - a1 * d1)
                    rows = slice(i * channels + g * 16, i * channels + (g + 1) * 16)
                    buf[rows, j * 128:(j + 1) * 128] = real
                    buf[rows, F + j * 128:F + (j + 1) * 128] = imag

    def lags(base, buf):
        res = jnp.dot(buf[...], inv_ref[...], preferred_element_type=jnp.float32)
        out_buf[pl.ds(pl.multiple_of(base, SUB), SUB)] = res.astype(jnp.bfloat16).reshape(SUB, channels, LAGS)

    def copy_out(k):
        rows = pl.ds(k * 2 * SUB, 2 * SUB)
        return pltpu.make_async_copy(out_buf.at[rows], out_ref.at[rows], sems.at[k])

    steps = ROWS // (2 * SUB)
    cross(0, cross_a)

    @pl.loop(0, steps)
    def _(k):
        base = k * 2 * SUB
        lags(base, cross_a)
        cross(base + SUB, cross_b)
        lags(base + SUB, cross_b)
        cross(jnp.minimum(base + 2 * SUB, ROWS - SUB), cross_a)
        copy_out(k).start()

    @pl.loop(0, steps)
    def _(k):
        copy_out(k).wait()


def on_device(records, quality_mask, band_start):
    devices_col = lax.axis_size("col")
    position = lax.axis_index("col")
    channels = records.shape[0] // devices_col
    forward, inverse = dft_tables()
    first_row = band_start[0]
    local_time = records.shape[1]
    groups = local_time // 16
    n = devices_col
    vmem = pl.BlockSpec(memory_space=pltpu.VMEM)
    hbm = pl.BlockSpec(memory_space=pl.ANY)
    slab, pack = pl.pallas_call(
        functools.partial(prep_kernel, channels, groups),
        out_shape=(
            jax.ShapeDtypeStruct((2, local_time, ROWS // 2), jnp.bfloat16),
            jax.ShapeDtypeStruct((n, 16, 128), jnp.bfloat16),
        ),
        in_specs=[pl.BlockSpec(memory_space=pltpu.SMEM), vmem],
        out_specs=(vmem, vmem),
    )(band_start, records.T)
    band, own = pl.pallas_call(
        functools.partial(exchange_kernel, n),
        out_shape=(
            jax.ShapeDtypeStruct((2, n, local_time, ROWS // 2), jnp.bfloat16),
            jax.ShapeDtypeStruct((n, 16, 128), jnp.bfloat16),
        ),
        in_specs=[hbm, hbm],
        out_specs=(hbm, hbm),
        scratch_shapes=[
            pltpu.SemaphoreType.DMA((2, n)),
            pltpu.SemaphoreType.DMA((2, n)),
            pltpu.SemaphoreType.DMA((n,)),
            pltpu.SemaphoreType.DMA((n,)),
            pltpu.SemaphoreType.DMA((3,)),
        ],
        compiler_params=pltpu.CompilerParams(collective_id=0, has_side_effects=True),
    )(slab, pack)
    band = band.reshape(2, n * local_time, ROWS // 2)
    mask = quality_mask.astype(jnp.float32)
    keep_band = lax.dynamic_slice_in_dim(mask, first_row, ROWS, 0)[:, None]
    keep_own = lax.dynamic_slice_in_dim(mask, position * channels, channels, 0)[:, None]
    return pl.pallas_call(
        functools.partial(correlate_kernel, channels),
        out_shape=jax.ShapeDtypeStruct((ROWS, channels, LAGS), jnp.bfloat16),
        in_specs=[pl.BlockSpec(memory_space=pltpu.HBM)] + [vmem] * 5,
        out_specs=pl.BlockSpec(memory_space=pl.ANY),
        scratch_shapes=[
            pltpu.VMEM((ROWS, 4 * F), jnp.float32),
            pltpu.VMEM((channels, 4 * F), jnp.bfloat16),
            pltpu.VMEM((SUB * channels, 2 * F), jnp.bfloat16),
            pltpu.VMEM((SUB * channels, 2 * F), jnp.bfloat16),
            pltpu.VMEM((ROWS, channels, LAGS), jnp.bfloat16),
            pltpu.SemaphoreType.DMA((ROWS // (2 * SUB),)),
            pltpu.VMEM((2, SEG * L, ROWS // 2), jnp.bfloat16),
            pltpu.SemaphoreType.DMA((2,)),
        ],
        compiler_params=pltpu.CompilerParams(vmem_limit_bytes=52 * 2**20),
    )(band, own, keep_band, keep_own, jnp.asarray(forward), jnp.asarray(inverse))


def solution(mesh):
    return jax.shard_map(
        on_device,
        mesh=mesh,
        in_specs=(P("win", "col"), P("win"), P("win")),
        out_specs=P("win", "col", None),
        check_vma=False,
    )
```
